512 devices in a mesh: seq: 32 (over y, x), head: 16 (over z, core).
Axes of the slice: x: 4, y: 8, z: 8, core: 2. Of those that a mesh axis runs over, the one named last changes fastest.
Arguments:
- queries: bfloat16 [2048, 8192], P('seq', 'head'), may hold values from -6 to 6
- keys: bfloat16 [2048, 1024], P('seq'), may hold values from -6 to 6
- values: bfloat16 [2048, 1024], P('seq'), may hold values from -6 to 6
- vertical: int32 [64, 8], replicated, may hold values from -1 to 31, as said below
- slash: int32 [64, 8], replicated, may hold values from -1 to 31, as said below
- plan: int32 [64], replicated, may hold values from 0 to 63, each once
Outputs:
- attended: bfloat16 [2048, 8192], P('seq', 'head')
The draws below stay inside these ranges and needn't reach their ends.
Inputs may be any that keep to these rules, and one draw needn't show every extreme that they name: `vertical`: entries of 0 or more name key blocks of 64 positions; -1 marks an unused entry, and every row has at least one used entry. `slash`: entries of 0 or more are offsets back from a query's own block; -1 marks an unused entry; the first entry of every row is 0. `plan`: A permutation of the query heads.
All inputs are finite; a program needn't handle non-finite values.
Results may differ from the reference program's by a relative error of at most 0.0044.
Values may be sent and summed in bfloat16 or wider, within the bound.
A program may use at most 64 MiB of HBM per device.

```python
import jax
import jax.numpy as jnp
from jax import lax

HD = 128
QH = 64
KVH = 8
BLK = 64
NV = 8
NS = 8
TOKENS = 2048


def draw_queries(key, part):
    key = jax.random.fold_in(key, 3)
    return jax.random.normal(key, (TOKENS, QH * HD), jnp.float32).astype(jnp.bfloat16)


def draw_keys(key, part):
    key = jax.random.fold_in(key, 5)
    return jax.random.normal(key, (TOKENS, KVH * HD), jnp.float32).astype(jnp.bfloat16)


def draw_vertical(key, part):
    key = jax.random.fold_in(key, 7)
    block_count = TOKENS // BLK
    count_key, entry_key, head_key = jax.random.split(key, 3)
    counts = jax.random.randint(count_key, (QH,), 1, NV)
    entries = jax.random.randint(entry_key, (QH, NV), 0, block_count)
    in_use = jnp.arange(NV)[None, :] < counts[:, None]
    listing = jnp.where(in_use, entries, -1)
    forced_head = jax.random.randint(head_key, (), 0, QH)
    return listing.at[forced_head, 0].set(block_count - 1).astype(jnp.int32)


def draw_slash(key, part):
    key = jax.random.fold_in(key, 9)
    block_count = TOKENS // BLK
    count_key, entry_key, head_key = jax.random.split(key, 3)
    counts = jax.random.randint(count_key, (QH,), 2, NS)
    entries = jax.random.randint(entry_key, (QH, NS), 0, block_count)
    in_use = jnp.arange(NS)[None, :] < counts[:, None]
    listing = jnp.where(in_use, entries, -1)
    listing = listing.at[:, 0].set(0)
    forced_head = jax.random.randint(head_key, (), 0, QH)
    return listing.at[forced_head, 1].set(block_count - 1).astype(jnp.int32)


def level_of(own_key, shape, shards, least, high):
    factor_of = 1.0
    for dim, shards_of in shards:
        steps = jax.random.uniform(jax.random.fold_in(jax.random.fold_in(own_key, 6), dim), (shards_of,), jnp.float32, least / len(shards), high / len(shards))
        factor_of = factor_of * jnp.repeat(jnp.exp(steps), shape[dim] // shards_of).reshape((-1,) + (1,) * (len(shape) - 1 - dim))
    return factor_of


def normal_values(key, dims, spread, most, cuts=(), kind=jnp.bfloat16):
    level = level_of(key, dims, cuts, -0.22, 0.18) if cuts else 1.0
    values = jax.random.normal(key, dims, jnp.float32) * spread * level
    return jnp.minimum(jnp.maximum(values, -most), most).astype(kind)


def setup_inputs(seed: int = 0) -> dict:
    key_of = jax.random.split(jax.random.key(seed), 7)
    queries = draw_queries(jax.random.fold_in(key_of[6], 71), 0)
    keys = draw_keys(jax.random.fold_in(key_of[6], 71), 0)
    values = normal_values(key_of[2], (TOKENS, KVH * HD), 1.0, 6.0, ((0, 32),))
    vertical = draw_vertical(jax.random.fold_in(key_of[6], 71), 0)
    slash = draw_slash(jax.random.fold_in(key_of[6], 71), 0)
    plan = jax.random.permutation(key_of[5], QH).astype(jnp.int32)
    return dict(queries=queries, keys=keys, values=values, vertical=vertical, slash=slash, plan=plan)


def head_attention(queries3, keys3, values3, head_id, vertical_row, slash_row):
    kv_head = head_id * KVH // QH
    query_rows = jnp.take(queries3, head_id, axis=1).astype(jnp.float32)
    key_rows = jnp.take(keys3, kv_head, axis=1).astype(jnp.float32)
    value_rows = jnp.take(values3, kv_head, axis=1).astype(jnp.float32)
    block_count = TOKENS // BLK
    own_blocks = jnp.arange(block_count, dtype=jnp.int32)
    slash_blocks = own_blocks[:, None] - slash_row[None, :]
    vert_blocks = jnp.broadcast_to(vertical_row[None, :], (block_count, NV))
    candidate = jnp.concatenate([vert_blocks, slash_blocks], axis=1)
    usable = jnp.concatenate([vert_blocks >= 0, (slash_row[None, :] >= 0) & (slash_blocks >= 0)], axis=1)
    list_width = NV + NS
    earlier = jnp.arange(list_width)[:, None] > jnp.arange(list_width)[None, :]
    repeated = jnp.any(earlier[None] & usable[:, None, :] & (candidate[:, :, None] == candidate[:, None, :]), axis=2)
    usable = usable & jnp.logical_not(repeated)
    clipped = jnp.clip(candidate, 0, block_count - 1).astype(jnp.int32)
    key_blocks = key_rows.reshape(block_count, BLK, HD)[clipped]
    value_blocks = value_rows.reshape(block_count, BLK, HD)[clipped]
    query_blocks = query_rows.reshape(block_count, BLK, HD)
    scores = jnp.einsum("bqh,bckh->bqck", query_blocks, key_blocks) * (HD ** -0.5)
    query_pos = own_blocks[:, None] * BLK + jnp.arange(BLK, dtype=jnp.int32)[None, :]
    key_pos = clipped[:, :, None] * BLK + jnp.arange(BLK, dtype=jnp.int32)[None, None, :]
    allowed = usable[:, None, :, None] & (key_pos[:, None, :, :] <= query_pos[:, :, None, None])
    masked = jnp.where(allowed, scores, -1e30)
    row_max = jnp.max(masked, axis=(2, 3), keepdims=True)
    weights = jnp.where(allowed, jnp.exp(masked - row_max), 0.0)
    totals = jnp.sum(weights, axis=(2, 3))
    rounded = lax.optimization_barrier(weights.astype(jnp.bfloat16)).astype(jnp.float32)
    mixture = jnp.einsum("bqck,bckh->bqh", rounded, value_blocks)
    return (mixture / totals[:, :, None]).reshape(TOKENS, HD)


def reference(queries, keys, values, vertical, slash, plan):
    queries3 = queries.reshape(TOKENS, QH, HD)
    keys3 = keys.reshape(TOKENS, KVH, HD)
    values3 = values.reshape(TOKENS, KVH, HD)

    def one_slot(slot_id):
        head_id = plan[slot_id]
        return head_attention(queries3, keys3, values3, head_id, vertical[head_id], slash[head_id])

    results = lax.map(one_slot, jnp.arange(QH, dtype=jnp.int32))
    return jnp.transpose(results, (1, 0, 2)).reshape(TOKENS, QH * HD).astype(jnp.bfloat16)
```

```python
import functools

import jax
import jax.numpy as jnp
from jax import lax
from jax.experimental import pallas as pl
from jax.experimental.pallas import tpu as pltpu
from jax.sharding import PartitionSpec as P

HD = 128
BLK = 64
HALF = BLK // 2
NX = 4
GROUP = 8
OWN = 4
LOW = -1e30
SCALE2 = (HD**-0.5) * 1.4426950408889634
MESH = pl.DeviceIdType.MESH


def kernel(
    ny, nx, nz,
    plan, vertical, slash, queries, keys, values, out,
    kvb, qb, qs, vt, scores, weights, bias, peak, part, got, gath, pick, rest,
    in_sem, y_send, x_send, kv_recv, q_sem, part_sem, z_send, z_recv, rest_sem,
):
    s = lax.axis_index("seq")
    h = lax.axis_index("head")
    y, x = s // nx, s % nx
    z, core = h // 2, h % 2
    sib = z * 2 + (1 - core)
    rows = GROUP * BLK

    kvb[...] = jnp.zeros_like(kvb)
    column = pl.ds(pl.multiple_of(z * HD, HD), HD)
    half = pl.ds(pl.multiple_of(core * HALF, HALF), HALF)
    loads = [
        pltpu.make_async_copy(keys.at[half, column], kvb.at[s, 0], in_sem.at[0]),
        pltpu.make_async_copy(values.at[half, column], kvb.at[s, 1], in_sem.at[1]),
        pltpu.make_async_copy(queries, qb.at[core], in_sem.at[2]),
    ]
    for load in loads:
        load.start()

    barrier = pltpu.get_barrier_semaphore()
    partners = [((y + t) % ny * nx + x, h) for t in range(1, ny)]
    partners += [(y * nx + (x + t) % nx, h) for t in range(1, nx)]
    partners += [(s, sib)]
    partners += [(s, (z + 1) % nz * 2 + core)]
    if nz > 2:
        partners += [(s, (z + nz - 1) % nz * 2 + core)]
    for partner in partners:
        pl.semaphore_signal(barrier, inc=1, device_id=partner, device_id_type=MESH)
    pl.semaphore_wait(barrier, len(partners))

    for load in loads:
        load.wait()

    def y_copy(t):
        return pltpu.make_async_remote_copy(
            src_ref=kvb.at[s], dst_ref=kvb.at[s], send_sem=y_send.at[t - 1], recv_sem=kv_recv.at[s],
            device_id=((y + t) * nx + x, h), device_id_type=MESH)

    def x_copy(row, t):
        b = row * nx + x
        return pltpu.make_async_remote_copy(
            src_ref=kvb.at[b], dst_ref=kvb.at[b], send_sem=x_send.at[row, t - 1], recv_sem=kv_recv.at[b],
            device_id=(y * nx + (x + t) % nx, h), device_id_type=MESH)

    def block_wait(b):
        pltpu.make_async_remote_copy(
            src_ref=kvb.at[b], dst_ref=kvb.at[b], send_sem=y_send.at[0], recv_sem=kv_recv.at[b],
            device_id=(s, sib), device_id_type=MESH).wait_recv()

    for t in range(1, ny):
        @pl.when(y + t < ny)
        def _():
            y_copy(t).start()
    for t in range(1, nx):
        x_copy(y, t).start()
    q_copy = pltpu.make_async_remote_copy(
        src_ref=qb.at[core], dst_ref=qb.at[core], send_sem=q_sem.at[0], recv_sem=q_sem.at[1],
        device_id=(s, sib), device_id_type=MESH)
    q_copy.start()

    head_rows = pl.ds(pl.multiple_of(z * GROUP, GROUP), GROUP)
    spread = (
        lax.broadcasted_iota(jnp.int32, (GROUP, rows), 0)
        == lax.broadcasted_iota(jnp.int32, (GROUP, rows), 1) // BLK
    ).astype(jnp.float32)

    def by_row(table):
        return lax.dot_general(
            table[head_rows, :].astype(jnp.float32), spread, (((0,), (0,)), ((), ())),
            preferred_element_type=jnp.float32)

    vert_rows = by_row(vertical)
    slash_rows = by_row(slash)
    blocks = lax.broadcasted_iota(jnp.int32, (ny * nx, rows), 0)
    block_f = blocks.astype(jnp.float32)
    gap_f = (s - blocks).astype(jnp.float32)
    hit = block_f < 0
    for n in range(vert_rows.shape[0]):
        hit = hit | (block_f == vert_rows[n : n + 1, :])
    for n in range(slash_rows.shape[0]):
        hit = hit | (gap_f == slash_rows[n : n + 1, :])
    bias[...] = jnp.where(hit & (blocks <= s), 0.0, LOW)

    for t in range(1, ny):
        @pl.when(y - t >= 0)
        def _():
            row = y - t
            block_wait(row * nx + x)
            for u in range(1, nx):
                x_copy(row, u).start()

    q_copy.wait()
    for i in range(GROUP):
        qs[i * BLK : (i + 1) * BLK, :] = qb[i // OWN, :, (i % OWN) * HD : (i % OWN + 1) * HD]

    peak[...] = jnp.full_like(peak, LOW)
    chunk = nx * HALF
    for row in range(ny):
        at = slice(row * chunk, (row + 1) * chunk)

        @pl.when(row <= y)
        def _():
            for u in range(1, nx):
                block_wait(row * nx + (x + u) % nx)
            k_rows = kvb[row * nx : (row + 1) * nx, 0].reshape(chunk, HD)
            v_rows = kvb[row * nx : (row + 1) * nx, 1].reshape(chunk, HD)
            vt[:, at] = v_rows.astype(jnp.float32).T.astype(jnp.bfloat16)
            raw = lax.dot_general(
                k_rows, qs[...], (((1,), (1,)), ((), ())), preferred_element_type=jnp.float32)
            raw = raw.reshape(nx, HALF, rows) + bias[row * nx : (row + 1) * nx, :].reshape(nx, 1, rows)
            shape = (nx, HALF, rows)
            key_at = (
                (row * nx + lax.broadcasted_iota(jnp.int32, shape, 0)) * BLK
                + core * HALF + lax.broadcasted_iota(jnp.int32, shape, 1))
            query_at = s * BLK + lax.broadcasted_iota(jnp.int32, shape, 2) % BLK
            raw = jnp.where(key_at <= query_at, raw, LOW).reshape(chunk, rows)
            scores[at, :] = raw
            peak[...] = jnp.maximum(peak[...], jnp.max(raw.reshape(chunk // 8, 8, rows), axis=0))

        @pl.when(row > y)
        def _():
            vt[:, at] = jnp.zeros((HD, chunk), jnp.bfloat16)
            weights[at, :] = jnp.zeros((chunk, rows), jnp.bfloat16)

    top = jnp.max(peak[...], axis=0, keepdims=True)
    peak[...] = jnp.zeros_like(peak)
    for row in range(ny):
        at = slice(row * chunk, (row + 1) * chunk)

        @pl.when(row <= y)
        def _():
            w = jnp.exp2((scores[at, :] - top) * SCALE2)
            peak[...] += jnp.sum(w.reshape(chunk // 8, 8, rows), axis=0)
            weights[at, :] = w.astype(jnp.bfloat16)

    total = jnp.sum(peak[...], axis=0, keepdims=True)
    sums = lax.dot_general(
        vt[...], weights[...], (((1,), (0,)), ((), ())), preferred_element_type=jnp.float32)
    mine = OWN * BLK
    for c in range(2):
        lanes = slice(c * mine, (c + 1) * mine)
        part[c, :HD, :] = sums[:, lanes]
        part[c, HD : HD + 8, :] = jnp.broadcast_to(top[:, lanes], (8, mine))
        part[c, HD + 8 :, :] = jnp.broadcast_to(total[:, lanes], (8, mine))
    part_copy = pltpu.make_async_remote_copy(
        src_ref=part.at[1 - core], dst_ref=got, send_sem=part_sem.at[0], recv_sem=part_sem.at[1],
        device_id=(s, sib), device_id_type=MESH)
    part_copy.start()
    part_copy.wait_recv()
    top_a, top_b = part[core, HD : HD + 1, :], got[HD : HD + 1, :]
    both = jnp.maximum(top_a, top_b)
    scale_a = jnp.exp2((top_a - both) * SCALE2)
    scale_b = jnp.exp2((top_b - both) * SCALE2)
    under = part[core, HD + 8 : HD + 9, :] * scale_a + got[HD + 8 : HD + 9, :] * scale_b
    mixed = (part[core, :HD, :] * scale_a + got[:HD, :] * scale_b) / under
    gath[z] = mixed.T.astype(jnp.bfloat16).reshape(OWN, BLK, HD)

    far = nz // 2
    pieces = [(0, 0, far), (0, 1, far - 1), (1, 1, far), (1, 0, far - 1)]

    def z_copy(way, piece, hop):
        step = 1 if way == 0 else nz - 1
        owner = (z + (nz - 1 if way == 0 else 1) * (hop - 1)) % nz
        block = gath.at[owner, pl.ds(piece * 2, 2)]
        return pltpu.make_async_remote_copy(
            src_ref=block, dst_ref=block, send_sem=z_send.at[way, piece, hop - 1],
            recv_sem=z_recv.at[way, piece, hop - 1],
            device_id=(s, (z + step) % nz * 2 + core), device_id_type=MESH)

    def z_wait(way, piece, hop):
        owner = (z + (nz - 1 if way == 0 else 1) * hop) % nz
        block = gath.at[owner, pl.ds(piece * 2, 2)]
        pltpu.make_async_remote_copy(
            src_ref=block, dst_ref=block, send_sem=z_send.at[way, piece, hop - 1],
            recv_sem=z_recv.at[way, piece, hop - 1],
            device_id=(s, sib), device_id_type=MESH).wait_recv()

    for hop in range(1, far + 1):
        for way, piece, hops in pieces:
            if hop <= hops:
                if hop > 1:
                    z_wait(way, piece, hop - 1)
                z_copy(way, piece, hop).start()
    for way, piece, hops in pieces:
        if hops:
            z_wait(way, piece, hops)

    for t in range(OWN):
        head = plan[sib * OWN + t]
        pick[t] = gath[head // GROUP, head % OWN]
    rest_copy = pltpu.make_async_remote_copy(
        src_ref=pick, dst_ref=rest, send_sem=rest_sem.at[0], recv_sem=rest_sem.at[1],
        device_id=(s, sib), device_id_type=MESH)
    rest_copy.start()
    rest_copy.wait_recv()
    for t in range(OWN):
        head = plan[h * OWN + t]
        here = (head // OWN) % 2 == core
        out[:, t * HD : (t + 1) * HD] = jnp.where(here, gath[head // GROUP, head % OWN], rest[t])

    for t in range(1, ny):
        @pl.when(y + t < ny)
        def _():
            y_copy(t).wait_send()
    for row in range(ny):
        @pl.when(row <= y)
        def _():
            for u in range(1, nx):
                x_copy(row, u).wait_send()
    part_copy.wait_send()
    for way, piece, hops in pieces:
        for hop in range(1, hops + 1):
            z_copy(way, piece, hop).wait_send()
    rest_copy.wait_send()


def per_device(nx, queries, keys, values, vertical, slash, plan):
    nz = lax.axis_size("head") // 2
    ny = lax.axis_size("seq") // nx
    nb = ny * nx
    rows = GROUP * BLK
    mine = OWN * BLK
    half_keys = nb * HALF
    far = nz // 2
    bf, f32 = jnp.bfloat16, jnp.float32
    vmem = pl.BlockSpec(memory_space=pltpu.VMEM)
    smem = pl.BlockSpec(memory_space=pltpu.SMEM)
    anywhere = pl.BlockSpec(memory_space=pl.ANY)
    dma = pltpu.SemaphoreType.DMA
    return pl.pallas_call(
        functools.partial(kernel, ny, nx, nz),
        out_shape=jax.ShapeDtypeStruct((BLK, OWN * HD), bf),
        in_specs=[smem, vmem, vmem, anywhere, anywhere, anywhere],
        out_specs=vmem,
        scratch_shapes=[
            pltpu.VMEM((nb, 2, HALF, HD), bf),
            pltpu.VMEM((2, BLK, OWN * HD), bf),
            pltpu.VMEM((rows, HD), bf),
            pltpu.VMEM((HD, half_keys), bf),
            pltpu.VMEM((half_keys, rows), f32),
            pltpu.VMEM((half_keys, rows), bf),
            pltpu.VMEM((nb, rows), f32),
            pltpu.VMEM((8, rows), f32),
            pltpu.VMEM((2, HD + 16, mine), f32),
            pltpu.VMEM((HD + 16, mine), f32),
            pltpu.VMEM((nz, OWN, BLK, HD), bf),
            pltpu.VMEM((OWN, BLK, HD), bf),
            pltpu.VMEM((OWN, BLK, HD), bf),
            dma((3,)),
            dma((ny,)),
            dma((ny, nx)),
            dma((nb,)),
            dma((2,)),
            dma((2,)),
            dma((2, 2, far)),
            dma((2, 2, far)),
            dma((2,)),
        ],
        compiler_params=pltpu.CompilerParams(
            collective_id=0, has_side_effects=True, vmem_limit_bytes=32 * 2**20),
    )(plan, vertical, slash, queries, keys, values)


def solution(mesh, nx=NX):
    in_specs = (P("seq", "head"), P("seq", None), P("seq", None), P(), P(), P())
    return jax.shard_map(
        functools.partial(per_device, nx), mesh=mesh, in_specs=in_specs,
        out_specs=P("seq", "head"), check_vma=False)
```

```python
import functools

import jax
import jax.numpy as jnp
from jax import lax
from jax.experimental import pallas as pl
from jax.experimental.pallas import tpu as pltpu
from jax.sharding import PartitionSpec as P

HD = 128
BLK = 64
HALF = BLK // 2
NX = 4
GROUP = 8
OWN = 4
LOW = -1e30
SCALE2 = (HD**-0.5) * 1.4426950408889634
MESH = pl.DeviceIdType.MESH


def kernel(
    ny, nx, nz,
    plan_hbm, vertical_hbm, slash_hbm, queries, keys, values, out,
    plan, vertical, slash, kvb, qb, qs, bias, top, total, part, got, gath, pick, rest,
    in_sem, y_send, far_send, across_send, x_send, kv_recv, q_sem, part_sem, z_send, pass_send, z_recv, rest_sem, late,
):
    s = lax.axis_index("seq")
    h = lax.axis_index("head")
    y, x = s // nx, s % nx
    z, core = h // 2, h % 2
    sib = z * 2 + (1 - core)
    ne = nz // 2
    early = z < ne
    rows = GROUP * BLK
    mine = OWN * BLK
    chunk = nx * HALF
    sides = [t for t in sorted({1, nx - 1}) if t % nx]
    across = nx // 2 if nx > 2 else 0

    def signal(where, device):
        pl.semaphore_signal(where, inc=1, device_id=device, device_id_type=MESH)

    def remote(src, dst, send, recv, device):
        return pltpu.make_async_remote_copy(
            src_ref=src, dst_ref=dst, send_sem=send, recv_sem=recv, device_id=device, device_id_type=MESH)

    column = pl.ds(pl.multiple_of(z * HD, HD), HD)
    half = pl.ds(pl.multiple_of(core * HALF, HALF), HALF)
    k_load = pltpu.make_async_copy(keys.at[half, column], kvb.at[s, 0], in_sem.at[0])
    v_load = pltpu.make_async_copy(values.at[half, column], kvb.at[s, 1], in_sem.at[1])
    q_load = pltpu.make_async_copy(queries, qb.at[core], in_sem.at[2])
    plan_load = pltpu.make_async_copy(plan_hbm, plan, in_sem.at[3])
    vert_load = pltpu.make_async_copy(vertical_hbm, vertical, in_sem.at[4])
    slash_load = pltpu.make_async_copy(slash_hbm, slash, in_sem.at[5])
    loads = [k_load, v_load, q_load, vert_load, slash_load, plan_load]
    for load in loads:
        load.start()

    barrier = pltpu.get_barrier_semaphore()
    partners = [((y + t) % ny * nx + x, h) for t in range(1, ny)]
    partners += [(y * nx + (x + t) % nx, h) for t in range(1, nx)]
    partners += [(s, sib)]
    for partner in partners:
        signal(barrier, partner)
    for other in range(1, nz):
        @pl.when(other > z)
        def _():
            signal(barrier, (s, other * 2 + core))
    pl.semaphore_wait(barrier, len(partners) + z)

    def y_copy(t):
        return remote(kvb.at[s], kvb.at[s], y_send.at[t - 1], kv_recv.at[s], ((y + t) * nx + x, h))

    over = y * nx + (x + across) % nx

    def far_copy(t):
        return remote(kvb.at[over], kvb.at[over], far_send.at[t - 1], kv_recv.at[over], ((y + t) * nx + x, h))

    across_copy = remote(kvb.at[s], kvb.at[s], across_send.at[0], kv_recv.at[s], (over, h))

    def x_copy(row, side):
        b = row * nx + x
        to = (x + sides[side]) % nx
        return remote(kvb.at[b], kvb.at[b], x_send.at[row, side], kv_recv.at[b], (y * nx + to, h))

    def block_wait(b):
        remote(kvb.at[b], kvb.at[b], y_send.at[0], kv_recv.at[b], (s, sib)).wait_recv()

    def above(t, action):
        @pl.when(y + t < ny)
        def _():
            action(t)

    k_load.wait()
    v_load.wait()
    if across:
        across_copy.start()
    for t in reversed(range(1, ny)):
        above(t, lambda t: y_copy(t).start())
    for side in range(len(sides)):
        x_copy(y, side).start()
    q_load.wait()
    q_copy = remote(qb.at[core], qb.at[core], q_sem.at[0], q_sem.at[1], (s, sib))
    q_copy.start()
    for other in range(nz - 1):
        @pl.when(other < z)
        def _():
            signal(late.at[z], (s, other * 2 + core))

    vert_load.wait()
    slash_load.wait()
    heads = vertical.shape[1]
    spread = (
        lax.broadcasted_iota(jnp.int32, (heads, rows), 0)
        == z * GROUP + lax.broadcasted_iota(jnp.int32, (heads, rows), 1) // BLK
    ).astype(jnp.float32)

    def by_row(table):
        return jnp.dot(table[...].astype(jnp.float32), spread, preferred_element_type=jnp.float32)

    vert_rows = by_row(vertical)
    slash_rows = by_row(slash)
    blocks = lax.broadcasted_iota(jnp.int32, (ny * nx, rows), 0)
    block_f = blocks.astype(jnp.float32)
    gap_f = (s - blocks).astype(jnp.float32)
    hit = block_f < 0
    for n in range(vert_rows.shape[0]):
        hit = hit | (block_f == vert_rows[n : n + 1, :])
    for n in range(slash_rows.shape[0]):
        hit = hit | (gap_f == slash_rows[n : n + 1, :])
    bias[...] = jnp.where(hit & (blocks <= s), 0.0, LOW).reshape(ny, nx, 1, rows)
    top[...] = jnp.full_like(top, LOW)
    total[...] = jnp.zeros_like(total)
    part[...] = jnp.zeros_like(part)

    nearest = sorted(range(1, ny), key=lambda t: min(t, ny - t))
    if across:
        block_wait(over)
        for t in reversed(range(1, ny)):
            above(t, lambda t: far_copy(t).start())
    for t in nearest:
        @pl.when(y - t >= 0)
        def _():
            block_wait((y - t) * nx + x)
            for side in range(len(sides)):
                x_copy(y - t, side).start()

    q_copy.wait()
    for i in range(GROUP):
        qs[i * BLK : (i + 1) * BLK, :] = qb[i // OWN, :, (i % OWN) * HD : (i % OWN + 1) * HD]

    def attend(row):
        these = pl.ds(row * nx, nx)
        k_rows = kvb[these, 0].reshape(chunk, HD)
        v_rows = kvb[these, 1].reshape(chunk, HD)
        v_turned = v_rows.astype(jnp.float32).T.astype(jnp.bfloat16)
        raw = lax.dot_general(
            k_rows, qs[...], (((1,), (1,)), ((), ())), preferred_element_type=jnp.float32)
        shape = (nx, HALF, rows)
        raw = raw.reshape(shape) + bias[row]
        key_at = (
            (row * nx + lax.broadcasted_iota(jnp.int32, shape, 0)) * BLK
            + core * HALF + lax.broadcasted_iota(jnp.int32, shape, 1))
        query_at = s * BLK + lax.broadcasted_iota(jnp.int32, shape, 2) % BLK
        raw = jnp.where(key_at <= query_at, raw, LOW).reshape(chunk, rows)
        old = top[...]
        new = jnp.maximum(old, jnp.max(raw, axis=0, keepdims=True))
        w = jnp.exp2((raw - new) * SCALE2)
        keep = jnp.exp2((old - new) * SCALE2)
        top[...] = new
        total[...] = total[...] * keep + jnp.sum(w, axis=0, keepdims=True)
        more = jnp.dot(v_turned, w.astype(jnp.bfloat16), preferred_element_type=jnp.float32)
        for c in range(2):
            lanes = slice(c * mine, (c + 1) * mine)
            part[c, :HD, :] = part[c, :HD, :] * keep[:, lanes] + more[:, lanes]

    def one_row(row):
        for u in sides:
            block_wait(row * nx + (x + u) % nx)
        if across:
            @pl.when(row < y)
            def _():
                block_wait(row * nx + (x + across) % nx)
        attend(row)

    one_row(y)
    for t in nearest:
        @pl.when(y - t >= 0)
        def _():
            one_row(y - t)

    for c in range(2):
        lanes = slice(c * mine, (c + 1) * mine)
        part[c, HD : HD + 8, :] = jnp.broadcast_to(top[:, lanes], (8, mine))
        part[c, HD + 8 :, :] = jnp.broadcast_to(total[:, lanes], (8, mine))
    part_copy = remote(part.at[1 - core], got, part_sem.at[0], part_sem.at[1], (s, sib))
    part_copy.start()
    part_copy.wait_recv()
    top_a, top_b = part[core, HD : HD + 1, :], got[HD : HD + 1, :]
    both = jnp.maximum(top_a, top_b)
    scale_a = jnp.exp2((top_a - both) * SCALE2)
    scale_b = jnp.exp2((top_b - both) * SCALE2)
    under = part[core, HD + 8 : HD + 9, :] * scale_a + got[HD + 8 : HD + 9, :] * scale_b
    mixed = (part[core, :HD, :] * scale_a + got[:HD, :] * scale_b) / under
    gath[z] = mixed.T.astype(jnp.bfloat16).reshape(OWN, BLK, HD)

    top_edge, low_edge = nz - 1, ne
    edges = [sorted({0, ne - 1}), sorted({low_edge, top_edge})]
    passes = ne >= 4
    upper = range(nz - ne // 2, nz) if passes else []
    lower = [source for source in range(ne, nz) if source not in upper]

    def send(source, target, sem):
        return remote(gath.at[source], gath.at[source], sem, z_recv.at[source], (s, target * 2 + core))

    def z_copy(target):
        return send(z, target, z_send.at[target])

    def pass_copy(source, target, lane=0):
        return send(source, target, pass_send.at[lane, source])

    def late_wait(target):
        @pl.when(target > z)
        def _():
            pl.semaphore_wait(late.at[target], 1)

    def arrive(source):
        @pl.when(source != z)
        def _():
            pass_copy(source, 0).wait_recv()

    routes = []
    if passes:
        routes += [(0, source, 1, 0) for source in reversed(upper)]
        for source in lower:
            routes += [(ne - 1, source, ne - 2, 0), (ne - 1, source, 1, 1)]
        routes += [(ne - 1, source, ne - 2, 0) for source in upper]
        routes += [(top_edge, source, top_edge - 1, 0) for source in range(ne)]
        routes += [(low_edge, source, low_edge + 1, 0) for source in range(ne)]

    def relay(plane, order):
        @pl.when(z == plane)
        def _():
            for source in order:
                arrive(source)
                for by, of, target, lane in routes:
                    if by == plane and of == source:
                        pass_copy(source, target, lane).start()

    @pl.when(early)
    def _():
        for target in range(ne):
            late_wait(target)

            @pl.when(target != z)
            def _():
                z_copy(target).start()
        for target in reversed(range(ne, nz)):
            late_wait(target)
            if target in edges[1]:
                z_copy(target).start()
        for source in range(ne):
            arrive(source)
        relay(0, list(reversed(range(ne, nz))))
        for plane in range(1, ne):
            relay(plane, list(range(ne, nz)))

    @pl.when(jnp.logical_not(early))
    def _():
        high = z >= nz - ne // 2
        if len(edges[0]) == 2:
            first = jnp.where(high, 0, ne - 1)
            second = ne - 1 - first
            send(z, first, z_send.at[0]).start()
            send(z, second, z_send.at[1]).start()
        else:
            send(z, 0, z_send.at[0]).start()
        for target in range(ne, nz):
            late_wait(target)

            @pl.when(target != z)
            def _():
                z_copy(target).start()
        for plane in range(ne, nz):
            relay(plane, list(range(ne)))
        for source in range(ne, nz):
            arrive(source)

    plan_load.wait()
    for t in range(OWN):
        head = plan[sib * OWN + t]
        pick[t] = gath[head // GROUP, head % OWN]
    rest_copy = remote(pick, rest, rest_sem.at[0], rest_sem.at[1], (s, sib))
    rest_copy.start()
    rest_copy.wait_recv()
    for t in range(OWN):
        head = plan[h * OWN + t]
        here = (head // OWN) % 2 == core
        out[:, t * HD : (t + 1) * HD] = jnp.where(here, gath[head // GROUP, head % OWN], rest[t])

    if across:
        across_copy.wait_send()
    for t in range(1, ny):
        above(t, lambda t: y_copy(t).wait_send())
        if across:
            above(t, lambda t: far_copy(t).wait_send())
    for row in range(ny):
        @pl.when(row <= y)
        def _():
            for side in range(len(sides)):
                x_copy(row, side).wait_send()
    part_copy.wait_send()

    @pl.when(early)
    def _():
        for target in range(ne):
            @pl.when(target != z)
            def _():
                z_copy(target).wait_send()
        for target in edges[1]:
            z_copy(target).wait_send()

    @pl.when(jnp.logical_not(early))
    def _():
        for target in range(len(edges[0])):
            z_copy(target).wait_send()
        for target in range(ne, nz):
            @pl.when(target != z)
            def _():
                z_copy(target).wait_send()
    for by, of, target, lane in routes:
        @pl.when(z == by)
        def _():
            pass_copy(of, target, lane).wait_send()
    rest_copy.wait_send()


def per_device(nx, queries, keys, values, vertical, slash, plan):
    nz = lax.axis_size("head") // 2
    ny = lax.axis_size("seq") // nx
    nb = ny * nx
    rows = GROUP * BLK
    mine = OWN * BLK
    bf, f32 = jnp.bfloat16, jnp.float32
    hbm = pl.BlockSpec(memory_space=pltpu.HBM)
    dma = pltpu.SemaphoreType.DMA
    tables = (vertical.shape[1], vertical.shape[0])
    return pl.pallas_call(
        functools.partial(kernel, ny, nx, nz),
        out_shape=jax.ShapeDtypeStruct((BLK, OWN * HD), bf),
        in_specs=[hbm] * 6,
        out_specs=pl.BlockSpec(memory_space=pltpu.VMEM),
        scratch_shapes=[
            pltpu.SMEM(plan.shape, jnp.int32),
            pltpu.VMEM(tables, jnp.int32),
            pltpu.VMEM(tables, jnp.int32),
            pltpu.VMEM((nb, 2, HALF, HD), bf),
            pltpu.VMEM((2, BLK, OWN * HD), bf),
            pltpu.VMEM((rows, HD), bf),
            pltpu.VMEM((ny, nx, 1, rows), f32),
            pltpu.VMEM((1, rows), f32),
            pltpu.VMEM((1, rows), f32),
            pltpu.VMEM((2, HD + 16, mine), f32),
            pltpu.VMEM((HD + 16, mine), f32),
            pltpu.VMEM((nz, OWN, BLK, HD), bf),
            pltpu.VMEM((OWN, BLK, HD), bf),
            pltpu.VMEM((OWN, BLK, HD), bf),
            dma((6,)),
            dma((ny,)),
            dma((ny,)),
            dma((1,)),
            dma((ny, 2)),
            dma((nb,)),
            dma((2,)),
            dma((2,)),
            dma((nz,)),
            dma((2, nz)),
            dma((nz,)),
            dma((2,)),
            pltpu.SemaphoreType.REGULAR((nz,)),
        ],
        compiler_params=pltpu.CompilerParams(
            collective_id=0, has_side_effects=True, vmem_limit_bytes=60 * 2**20),
    )(plan, vertical.T, slash.T, queries, keys, values)


def solution(mesh, nx=NX):
    in_specs = (P("seq", "head"), P("seq", None), P("seq", None), P(), P(), P())
    return jax.shard_map(
        functools.partial(per_device, nx), mesh=mesh, in_specs=in_specs,
        out_specs=P("seq", "head"), check_vma=False)
```

```python
import functools

import jax
import jax.numpy as jnp
from jax import lax
from jax.experimental import pallas as pl
from jax.experimental.pallas import tpu as pltpu
from jax.sharding import PartitionSpec as P

HD = 128
BLK = 64
HALF = BLK // 2
NX = 4
GROUP = 8
OWN = 4
LOW = -1e30
SCALE2 = (HD**-0.5) * 1.4426950408889634
MESH = pl.DeviceIdType.MESH


def kernel(
    ny, nx, nz,
    plan_hbm, vertical_hbm, slash_hbm, queries, keys, values, out, rest,
    plan, vertical, slash, kvb, qb, qs, bias, top, total, part, got, gath, pick, own,
    in_sem, y_send, far_send, across_send, x_send, kv_recv, q_sem, part_sem, z_send, pass_send, z_recv, rest_sem, late,
):
    s = lax.axis_index("seq")
    h = lax.axis_index("head")
    y, x = s // nx, s % nx
    z, core = h // 2, h % 2
    sib = z * 2 + (1 - core)
    ne = nz // 2
    early = z < ne
    rows = GROUP * BLK
    mine = OWN * BLK
    chunk = nx * HALF
    sides = [t for t in sorted({1, nx - 1}) if t % nx]
    across = nx // 2 if nx > 2 else 0

    def signal(where, device):
        pl.semaphore_signal(where, inc=1, device_id=device, device_id_type=MESH)

    def remote(src, dst, send, recv, device):
        return pltpu.make_async_remote_copy(
            src_ref=src, dst_ref=dst, send_sem=send, recv_sem=recv, device_id=device, device_id_type=MESH)

    column = pl.ds(pl.multiple_of(z * HD, HD), HD)
    half = pl.ds(pl.multiple_of(core * HALF, HALF), HALF)
    k_load = pltpu.make_async_copy(keys.at[half, column], kvb.at[s, 0], in_sem.at[0])
    v_load = pltpu.make_async_copy(values.at[half, column], kvb.at[s, 1], in_sem.at[1])
    q_load = pltpu.make_async_copy(queries, qb.at[core], in_sem.at[2])
    plan_load = pltpu.make_async_copy(plan_hbm, plan, in_sem.at[3])
    vert_load = pltpu.make_async_copy(vertical_hbm, vertical, in_sem.at[4])
    slash_load = pltpu.make_async_copy(slash_hbm, slash, in_sem.at[5])
    loads = [k_load, v_load, q_load, vert_load, slash_load, plan_load]
    for load in loads:
        load.start()

    barrier = pltpu.get_barrier_semaphore()
    partners = [(y * nx + (x + t) % nx, h) for t in range(1, nx)]
    partners += [(s, sib)]
    for partner in partners:
        signal(barrier, partner)

    def greet(row, carry):
        signal(barrier, (row * nx + x, h))
        return carry

    lax.fori_loop(0, y, greet, 0)
    for other in range(1, nz):
        @pl.when(other > z)
        def _():
            signal(barrier, (s, other * 2 + core))
    pl.semaphore_wait(barrier, len(partners) + ny - 1 - y + z)

    def y_copy(t):
        return remote(kvb.at[s], kvb.at[s], y_send.at[t - 1], kv_recv.at[s], ((y + t) * nx + x, h))

    over = y * nx + (x + across) % nx

    def far_copy(t):
        return remote(kvb.at[over], kvb.at[over], far_send.at[t - 1], kv_recv.at[over], ((y + t) * nx + x, h))

    across_copy = remote(kvb.at[s], kvb.at[s], across_send.at[0], kv_recv.at[s], (over, h))

    def x_copy(row, side):
        b = row * nx + x
        to = (x + sides[side]) % nx
        return remote(kvb.at[b], kvb.at[b], x_send.at[row, side], kv_recv.at[b], (y * nx + to, h))

    def block_wait(b):
        remote(kvb.at[b], kvb.at[b], y_send.at[0], kv_recv.at[b], (s, sib)).wait_recv()

    def above(action):
        def step(i, carry):
            action(ny - 1 - y - i)
            return carry

        lax.fori_loop(0, ny - 1 - y, step, 0)

    def below(action, first):
        def step(i, carry):
            t = jnp.where(i % 2 == 1, (i + 1) // 2, ny - i // 2) % ny

            @pl.when(t <= y)
            def _():
                action(y - t)

            return carry

        lax.fori_loop(first, ny, step, 0)

    k_load.wait()
    v_load.wait()
    if across:
        across_copy.start()
    above(lambda t: y_copy(t).start())
    for side in range(len(sides)):
        x_copy(y, side).start()
    q_load.wait()
    q_copy = remote(qb.at[core], qb.at[core], q_sem.at[0], q_sem.at[1], (s, sib))
    q_copy.start()
    for other in range(nz - 1):
        @pl.when(other < z)
        def _():
            signal(late.at[z], (s, other * 2 + core))

    vert_load.wait()
    slash_load.wait()
    heads = vertical.shape[1]
    spread = (
        lax.broadcasted_iota(jnp.int32, (heads, rows), 0)
        == z * GROUP + lax.broadcasted_iota(jnp.int32, (heads, rows), 1) // BLK
    ).astype(jnp.float32)
    blocks = lax.broadcasted_iota(jnp.int32, (ny * nx, heads), 0)
    hit = blocks < 0
    for n in range(vertical.shape[0]):
        hit = hit | (blocks == vertical[n : n + 1, :])
    for n in range(slash.shape[0]):
        hit = hit | (s - blocks == slash[n : n + 1, :])
    open_ = jnp.where(hit & (blocks <= s), 1.0, 0.0)
    open_rows = jnp.dot(open_, spread, preferred_element_type=jnp.float32)
    bias[...] = jnp.where(open_rows > 0.5, 0.0, LOW).reshape(ny, nx, 1, rows)
    top[...] = jnp.full_like(top, LOW)
    total[...] = jnp.zeros_like(total)
    part[...] = jnp.zeros_like(part)

    if across:
        @pl.when(core == 0)
        def _():
            block_wait(over)
            above(lambda t: far_copy(t).start())

    def wide_copy(row):
        b = row * nx + x
        return remote(kvb.at[b], kvb.at[b], far_send.at[row], kv_recv.at[b], (over, h))

    def forward(row):
        block_wait(row * nx + x)
        if across:
            @pl.when(core == 1)
            def _():
                wide_copy(row).start()
        for side in range(len(sides)):
            x_copy(row, side).start()

    below(forward, 1)

    q_copy.wait()
    for i in range(GROUP):
        qs[i * BLK : (i + 1) * BLK, :] = qb[i // OWN, :, (i % OWN) * HD : (i % OWN + 1) * HD]

    def attend(row):
        these = pl.ds(row * nx, nx)
        k_rows = kvb[these, 0].reshape(chunk, HD)
        v_rows = kvb[these, 1].reshape(chunk, HD)
        v_turned = v_rows.astype(jnp.float32).T.astype(jnp.bfloat16)
        raw = lax.dot_general(
            k_rows, qs[...], (((1,), (1,)), ((), ())), preferred_element_type=jnp.float32)
        shape = (nx, HALF, rows)
        raw = raw.reshape(shape) + bias[row]
        key_at = (
            (row * nx + lax.broadcasted_iota(jnp.int32, shape, 0)) * BLK
            + core * HALF + lax.broadcasted_iota(jnp.int32, shape, 1))
        query_at = s * BLK + lax.broadcasted_iota(jnp.int32, shape, 2) % BLK
        raw = jnp.where(key_at <= query_at, raw, LOW).reshape(chunk, rows)
        old = top[...]
        new = jnp.maximum(old, jnp.max(raw, axis=0, keepdims=True))
        w = jnp.exp2((raw - new) * SCALE2)
        keep = jnp.exp2((old - new) * SCALE2)
        top[...] = new
        total[...] = total[...] * keep + jnp.sum(w, axis=0, keepdims=True)
        more = jnp.dot(v_turned, w.astype(jnp.bfloat16), preferred_element_type=jnp.float32)
        for c in range(2):
            lanes = slice(c * mine, (c + 1) * mine)
            part[c, :HD, :] = part[c, :HD, :] * keep[:, lanes] + more[:, lanes]

    def one_row(row):
        for u in sides:
            block_wait(row * nx + (x + u) % nx)
        if across:
            @pl.when((row < y) | (core == 1))
            def _():
                block_wait(row * nx + (x + across) % nx)
        attend(row)

    below(one_row, 0)

    for c in range(2):
        lanes = slice(c * mine, (c + 1) * mine)
        part[c, HD : HD + 8, :] = jnp.broadcast_to(top[:, lanes], (8, mine))
        part[c, HD + 8 :, :] = jnp.broadcast_to(total[:, lanes], (8, mine))
    part_copy = remote(part.at[1 - core], got, part_sem.at[0], part_sem.at[1], (s, sib))
    part_copy.start()
    part_copy.wait_recv()
    top_a, top_b = part[core, HD : HD + 1, :], got[HD : HD + 1, :]
    both = jnp.maximum(top_a, top_b)
    scale_a = jnp.exp2((top_a - both) * SCALE2)
    scale_b = jnp.exp2((top_b - both) * SCALE2)
    under = part[core, HD + 8 : HD + 9, :] * scale_a + got[HD + 8 : HD + 9, :] * scale_b
    mixed = (part[core, :HD, :] * scale_a + got[:HD, :] * scale_b) / under
    gath[z] = mixed.T.astype(jnp.bfloat16).reshape(OWN, BLK, HD)

    top_edge, low_edge = nz - 1, ne
    edges = [sorted({0, ne - 1}), sorted({low_edge, top_edge})]
    passes = ne >= 4
    upper = range(nz - ne // 2, nz) if passes else []
    lower = [source for source in range(ne, nz) if source not in upper]

    def send(source, target, sem):
        return remote(gath.at[source], gath.at[source], sem, z_recv.at[source], (s, target * 2 + core))

    def z_copy(target):
        return send(z, target, z_send.at[target])

    def pass_copy(source, target, lane=0):
        return send(source, target, pass_send.at[lane, source])

    def late_wait(target):
        @pl.when(target > z)
        def _():
            pl.semaphore_wait(late.at[target], 1)

    def arrive(source):
        @pl.when(source != z)
        def _():
            pass_copy(source, 0).wait_recv()

    routes = []
    if passes:
        for source in upper:
            routes += [(0, source, 1, 0), (0, source, ne - 2, 1)]
        for source in lower:
            routes += [(ne - 1, source, ne - 2, 0), (ne - 1, source, 1, 1)]
        routes += [(top_edge, source, top_edge - 1, 0) for source in range(ne)]
        routes += [(low_edge, source, low_edge + 1, 0) for source in range(ne)]

    def relay(plane, order):
        @pl.when(z == plane)
        def _():
            for source in order:
                arrive(source)
                for by, of, target, lane in routes:
                    if by == plane and of == source:
                        pass_copy(source, target, lane).start()

    @pl.when(early)
    def _():
        for target in range(ne):
            late_wait(target)

            @pl.when(target != z)
            def _():
                z_copy(target).start()
        for target in reversed(range(ne, nz)):
            late_wait(target)
            if target in edges[1]:
                z_copy(target).start()
        for source in range(ne):
            arrive(source)
        relay(0, list(reversed(range(ne, nz))))
        for plane in range(1, ne):
            relay(plane, list(range(ne, nz)))

    @pl.when(jnp.logical_not(early))
    def _():
        high = z >= nz - ne // 2
        if len(edges[0]) == 2:
            first = jnp.where(high, 0, ne - 1)
            second = ne - 1 - first
            send(z, first, z_send.at[0]).start()
            for target in range(ne, nz):
                late_wait(target)

                @pl.when(target != z)
                def _():
                    z_copy(target).start()
            z_copy(0).wait_send()
            send(z, second, z_send.at[1]).start()
        else:
            send(z, 0, z_send.at[0]).start()
        for plane in range(ne, nz):
            relay(plane, list(range(ne)))
        for source in range(ne, nz):
            arrive(source)

    plan_load.wait()

    def collect(into, device):
        for t in range(OWN):
            head = plan[device * OWN + t]
            item = gath[head // GROUP, head % OWN]
            into[:, t * HD : (t + 1) * HD] = jnp.where((head // OWN) % 2 == core, item, jnp.zeros_like(item))

    collect(pick, sib)
    rest_copy = remote(pick, rest, rest_sem.at[0], rest_sem.at[1], (s, sib))
    rest_copy.start()
    collect(own, h)
    own_copy = pltpu.make_async_copy(own, out, in_sem.at[0])
    own_copy.start()

    if across:
        across_copy.wait_send()
    above(lambda t: y_copy(t).wait_send())
    if across:
        @pl.when(core == 0)
        def _():
            above(lambda t: far_copy(t).wait_send())

        @pl.when(core == 1)
        def _():
            below(lambda row: wide_copy(row).wait_send(), 1)

    def left(row):
        for side in range(len(sides)):
            x_copy(row, side).wait_send()

    below(left, 0)
    part_copy.wait_send()

    @pl.when(early)
    def _():
        for target in range(ne):
            @pl.when(target != z)
            def _():
                z_copy(target).wait_send()
        for target in edges[1]:
            z_copy(target).wait_send()

    @pl.when(jnp.logical_not(early))
    def _():
        z_copy(len(edges[0]) - 1).wait_send()
        for target in range(ne, nz):
            @pl.when(target != z)
            def _():
                z_copy(target).wait_send()
    for by, of, target, lane in routes:
        @pl.when(z == by)
        def _():
            pass_copy(of, target, lane).wait_send()
    rest_copy.wait()
    own_copy.wait()


def per_device(nx, queries, keys, values, vertical, slash, plan):
    nz = lax.axis_size("head") // 2
    ny = lax.axis_size("seq") // nx
    nb = ny * nx
    rows = GROUP * BLK
    mine = OWN * BLK
    bf, f32 = jnp.bfloat16, jnp.float32
    hbm = pl.BlockSpec(memory_space=pltpu.HBM)
    dma = pltpu.SemaphoreType.DMA
    tables = (vertical.shape[1], vertical.shape[0])
    out, rest = pl.pallas_call(
        functools.partial(kernel, ny, nx, nz),
        out_shape=[jax.ShapeDtypeStruct((BLK, OWN * HD), bf)] * 2,
        in_specs=[hbm] * 6,
        out_specs=[hbm] * 2,
        scratch_shapes=[
            pltpu.SMEM(plan.shape, jnp.int32),
            pltpu.VMEM(tables, jnp.int32),
            pltpu.VMEM(tables, jnp.int32),
            pltpu.VMEM((nb, 2, HALF, HD), bf),
            pltpu.VMEM((2, BLK, OWN * HD), bf),
            pltpu.VMEM((rows, HD), bf),
            pltpu.VMEM((ny, nx, 1, rows), f32),
            pltpu.VMEM((1, rows), f32),
            pltpu.VMEM((1, rows), f32),
            pltpu.VMEM((2, HD + 16, mine), f32),
            pltpu.VMEM((HD + 16, mine), f32),
            pltpu.VMEM((nz, OWN, BLK, HD), bf),
            pltpu.VMEM((BLK, OWN * HD), bf),
            pltpu.VMEM((BLK, OWN * HD), bf),
            dma((6,)),
            dma((ny,)),
            dma((ny,)),
            dma((1,)),
            dma((ny, 2)),
            dma((nb,)),
            dma((2,)),
            dma((2,)),
            dma((nz,)),
            dma((2, nz)),
            dma((nz,)),
            dma((2,)),
            pltpu.SemaphoreType.REGULAR((nz,)),
        ],
        compiler_params=pltpu.CompilerParams(
            collective_id=0, has_side_effects=True, vmem_limit_bytes=60 * 2**20),
    )(plan, vertical.T, slash.T, queries, keys, values)
    return out + rest


def solution(mesh, nx=NX):
    in_specs = (P("seq", "head"), P("seq", None), P("seq", None), P(), P(), P())
    return jax.shard_map(
        functools.partial(per_device, nx), mesh=mesh, in_specs=in_specs,
        out_specs=P("seq", "head"), check_vma=False)
```

```python
import functools

import jax
import jax.numpy as jnp
from jax import lax
from jax.experimental import pallas as pl
from jax.experimental.pallas import tpu as pltpu
from jax.sharding import PartitionSpec as P

HD = 128
BLK = 64
HALF = BLK // 2
NX = 4
GROUP = 8
OWN = 4
LOW = -1e30
SCALE2 = (HD**-0.5) * 1.4426950408889634
MESH = pl.DeviceIdType.MESH


def kernel(
    ny, nx, nz,
    plan_hbm, vertical_hbm, slash_hbm, queries, keys, values, out, rest,
    plan, vertical, slash, kvb, qb, qs, bias, top, total, part, got, gath, pick,
    in_sem, y_send, far_send, across_send, x_send, kv_recv, q_sem, part_sem, z_send, pass_send, z_recv, rest_sem, late,
):
    s = lax.axis_index("seq")
    h = lax.axis_index("head")
    y, x = s // nx, s % nx
    z, core = h // 2, h % 2
    sib = z * 2 + (1 - core)
    ne = nz // 2
    early = z < ne
    rows = GROUP * BLK
    mine = OWN * BLK
    chunk = nx * HALF
    sides = [t for t in sorted({1, nx - 1}) if t % nx]
    across = nx // 2 if nx > 2 else 0

    def signal(where, device):
        pl.semaphore_signal(where, inc=1, device_id=device, device_id_type=MESH)

    def remote(src, dst, send, recv, device):
        return pltpu.make_async_remote_copy(
            src_ref=src, dst_ref=dst, send_sem=send, recv_sem=recv, device_id=device, device_id_type=MESH)

    column = pl.ds(pl.multiple_of(z * HD, HD), HD)
    half = pl.ds(pl.multiple_of(core * HALF, HALF), HALF)
    k_load = pltpu.make_async_copy(keys.at[half, column], kvb.at[s, 0], in_sem.at[0])
    v_load = pltpu.make_async_copy(values.at[half, column], kvb.at[s, 1], in_sem.at[1])
    q_load = pltpu.make_async_copy(queries, qb.at[core], in_sem.at[2])
    plan_load = pltpu.make_async_copy(plan_hbm, plan, in_sem.at[3])
    vert_load = pltpu.make_async_copy(vertical_hbm, vertical, in_sem.at[4])
    slash_load = pltpu.make_async_copy(slash_hbm, slash, in_sem.at[5])
    loads = [k_load, v_load, q_load, vert_load, slash_load, plan_load]
    for load in loads:
        load.start()

    barrier = pltpu.get_barrier_semaphore()
    partners = [(y * nx + (x + t) % nx, h) for t in range(1, nx)]
    partners += [(s, sib)]
    for partner in partners:
        signal(barrier, partner)

    def greet(row, carry):
        signal(barrier, (row * nx + x, h))
        return carry

    lax.fori_loop(0, y, greet, 0)
    for other in range(1, nz):
        @pl.when(other > z)
        def _():
            signal(barrier, (s, other * 2 + core))
    pl.semaphore_wait(barrier, len(partners) + ny - 1 - y + z)

    def y_copy(t):
        return remote(kvb.at[s], kvb.at[s], y_send.at[t - 1], kv_recv.at[s], ((y + t) * nx + x, h))

    over = y * nx + (x + across) % nx

    def far_copy(t):
        return remote(kvb.at[over], kvb.at[over], far_send.at[t - 1], kv_recv.at[over], ((y + t) * nx + x, h))

    across_copy = remote(kvb.at[s], kvb.at[s], across_send.at[0], kv_recv.at[s], (over, h))

    def x_copy(row, side):
        b = row * nx + x
        to = (x + sides[side]) % nx
        return remote(kvb.at[b], kvb.at[b], x_send.at[row, side], kv_recv.at[b], (y * nx + to, h))

    def block_wait(b):
        remote(kvb.at[b], kvb.at[b], y_send.at[0], kv_recv.at[b], (s, sib)).wait_recv()

    def above(action):
        def step(i, carry):
            action(ny - 1 - y - i)
            return carry

        lax.fori_loop(0, ny - 1 - y, step, 0)

    def below(action, first):
        def step(i, carry):
            t = jnp.where(i % 2 == 1, (i + 1) // 2, ny - i // 2) % ny

            @pl.when(t <= y)
            def _():
                action(y - t)

            return carry

        lax.fori_loop(first, ny, step, 0)

    k_load.wait()
    v_load.wait()
    if across:
        across_copy.start()
    above(lambda t: y_copy(t).start())
    for side in range(len(sides)):
        x_copy(y, side).start()
    q_load.wait()
    q_copy = remote(qb.at[core], qb.at[core], q_sem.at[0], q_sem.at[1], (s, sib))
    q_copy.start()
    for other in range(nz - 1):
        @pl.when(other < z)
        def _():
            signal(late.at[z], (s, other * 2 + core))

    vert_load.wait()
    slash_load.wait()
    heads = vertical.shape[1]
    spread = (
        lax.broadcasted_iota(jnp.int32, (heads, rows), 0)
        == z * GROUP + lax.broadcasted_iota(jnp.int32, (heads, rows), 1) // BLK
    ).astype(jnp.float32)
    blocks = lax.broadcasted_iota(jnp.int32, (ny * nx, heads), 0)
    hit = blocks < 0
    for n in range(vertical.shape[0]):
        hit = hit | (blocks == vertical[n : n + 1, :])
    for n in range(slash.shape[0]):
        hit = hit | (s - blocks == slash[n : n + 1, :])
    open_ = jnp.where(hit & (blocks <= s), 1.0, 0.0)
    open_rows = jnp.dot(open_, spread, preferred_element_type=jnp.float32)
    bias[...] = jnp.where(open_rows > 0.5, 0.0, LOW).reshape(ny, nx, 1, rows)
    top[...] = jnp.full_like(top, LOW)
    total[...] = jnp.zeros_like(total)
    part[...] = jnp.zeros_like(part)

    if across:
        @pl.when(core == 0)
        def _():
            block_wait(over)
            above(lambda t: far_copy(t).start())

    def wide_copy(row):
        b = row * nx + x
        return remote(kvb.at[b], kvb.at[b], far_send.at[row], kv_recv.at[b], (over, h))

    def forward(row):
        block_wait(row * nx + x)
        if across:
            @pl.when(core == 1)
            def _():
                wide_copy(row).start()
        for side in range(len(sides)):
            x_copy(row, side).start()

    below(forward, 1)

    q_copy.wait()
    for i in range(GROUP):
        qs[i * BLK : (i + 1) * BLK, :] = qb[i // OWN, :, (i % OWN) * HD : (i % OWN + 1) * HD]

    def attend(row, diagonal):
        these = pl.ds(row * nx, nx)
        k_rows = kvb[these, 0].reshape(chunk, HD)
        v_rows = kvb[these, 1].reshape(chunk, HD)
        v_turned = v_rows.astype(jnp.float32).T.astype(jnp.bfloat16)
        raw = lax.dot_general(
            k_rows, qs[...], (((1,), (1,)), ((), ())), preferred_element_type=jnp.float32)
        shape = (nx, HALF, rows)
        raw = raw.reshape(shape) + bias[row]
        if diagonal:
            key_at = (
                (row * nx + lax.broadcasted_iota(jnp.int32, shape, 0)) * BLK
                + core * HALF + lax.broadcasted_iota(jnp.int32, shape, 1))
            query_at = s * BLK + lax.broadcasted_iota(jnp.int32, shape, 2) % BLK
            raw = jnp.where(key_at <= query_at, raw, LOW)
        raw = raw.reshape(chunk, rows)
        old = top[...]
        new = jnp.maximum(old, jnp.max(raw, axis=0, keepdims=True))
        w = jnp.exp2((raw - new) * SCALE2)
        keep = jnp.exp2((old - new) * SCALE2)
        top[...] = new
        total[...] = total[...] * keep + jnp.sum(w, axis=0, keepdims=True)
        more = jnp.dot(v_turned, w.astype(jnp.bfloat16), preferred_element_type=jnp.float32)
        for c in range(2):
            lanes = slice(c * mine, (c + 1) * mine)
            part[c, :HD, :] = part[c, :HD, :] * keep[:, lanes] + more[:, lanes]

    def one_row(row, diagonal=False):
        for u in sides:
            block_wait(row * nx + (x + u) % nx)
        if across:
            @pl.when((row < y) | (core == 1))
            def _():
                block_wait(row * nx + (x + across) % nx)
        attend(row, diagonal)

    one_row(y, True)
    below(one_row, 1)

    for c in range(2):
        lanes = slice(c * mine, (c + 1) * mine)
        part[c, HD : HD + 8, :] = jnp.broadcast_to(top[:, lanes], (8, mine))
        part[c, HD + 8 :, :] = jnp.broadcast_to(total[:, lanes], (8, mine))
    def part_copy(i):
        lanes = pl.ds(i * (mine // 2), mine // 2)
        return remote(part.at[1 - core, :, lanes], got.at[:, lanes], part_sem.at[0, i], part_sem.at[1, i], (s, sib))

    for i in range(2):
        part_copy(i).start()
    for i in range(2):
        lanes = slice(i * (mine // 2), (i + 1) * (mine // 2))
        part_copy(i).wait_recv()
        top_a, top_b = part[core, HD : HD + 1, lanes], got[HD : HD + 1, lanes]
        both = jnp.maximum(top_a, top_b)
        scale_a = jnp.exp2((top_a - both) * SCALE2)
        scale_b = jnp.exp2((top_b - both) * SCALE2)
        under = part[core, HD + 8 : HD + 9, lanes] * scale_a + got[HD + 8 : HD + 9, lanes] * scale_b
        mixed = part[core, :HD, lanes] * (scale_a / under) + got[:HD, lanes] * (scale_b / under)
        gath[z, i * 2 : i * 2 + 2] = mixed.T.astype(jnp.bfloat16).reshape(2, BLK, HD)

    top_edge, low_edge = nz - 1, ne
    edges = [sorted({0, ne - 1}), sorted({low_edge, top_edge})]
    passes = ne >= 4
    upper = range(nz - ne // 2, nz) if passes else []
    lower = [source for source in range(ne, nz) if source not in upper]

    def send(source, target, sem):
        return remote(gath.at[source], gath.at[source], sem, z_recv.at[source], (s, target * 2 + core))

    def z_copy(target):
        return send(z, target, z_send.at[target])

    def pass_copy(source, target, lane=0):
        return send(source, target, pass_send.at[lane, source])

    def late_wait(target):
        @pl.when(target > z)
        def _():
            pl.semaphore_wait(late.at[target], 1)

    def arrive(source):
        @pl.when(source != z)
        def _():
            pass_copy(source, 0).wait_recv()

    routes = []
    if passes:
        for source in upper:
            routes += [(0, source, 1, 0), (0, source, ne - 2, 1)]
        for source in lower:
            routes += [(ne - 1, source, ne - 2, 0), (ne - 1, source, 1, 1)]
        routes += [(top_edge, source, top_edge - 1, 0) for source in range(ne)]
        routes += [(low_edge, source, low_edge + 1, 0) for source in range(ne)]

    def relay(plane, order):
        @pl.when(z == plane)
        def _():
            for source in order:
                arrive(source)
                for by, of, target, lane in routes:
                    if by == plane and of == source:
                        pass_copy(source, target, lane).start()

    @pl.when(early)
    def _():
        for target in range(ne):
            late_wait(target)

            @pl.when(target != z)
            def _():
                z_copy(target).start()
        for target in reversed(range(ne, nz)):
            late_wait(target)
            if target in edges[1]:
                z_copy(target).start()
        for source in range(ne):
            arrive(source)
        relay(0, list(reversed(range(ne, nz))))
        for plane in range(1, ne):
            relay(plane, list(range(ne, nz)))

    @pl.when(jnp.logical_not(early))
    def _():
        high = z >= nz - ne // 2
        if len(edges[0]) == 2:
            first = jnp.where(high, 0, ne - 1)
            second = ne - 1 - first
            send(z, first, z_send.at[0]).start()
            for target in range(ne, nz):
                late_wait(target)

                @pl.when(target != z)
                def _():
                    z_copy(target).start()
            z_copy(0).wait_send()
            send(z, second, z_send.at[1]).start()
        else:
            send(z, 0, z_send.at[0]).start()
        for plane in range(ne, nz):
            relay(plane, list(range(ne)))
        for source in range(ne, nz):
            arrive(source)

    plan_load.wait()

    def collect(into, device):
        for t in range(OWN):
            head = plan[device * OWN + t]
            item = gath[head // GROUP, head % OWN]
            into[:, t * HD : (t + 1) * HD] = jnp.where((head // OWN) % 2 == core, item, jnp.zeros_like(item))

    collect(pick, sib)
    rest_copy = remote(pick, rest, rest_sem.at[0], rest_sem.at[1], (s, sib))
    rest_copy.start()
    collect(out, h)

    if across:
        across_copy.wait_send()
    above(lambda t: y_copy(t).wait_send())
    if across:
        @pl.when(core == 0)
        def _():
            above(lambda t: far_copy(t).wait_send())

        @pl.when(core == 1)
        def _():
            below(lambda row: wide_copy(row).wait_send(), 1)

    def left(row):
        for side in range(len(sides)):
            x_copy(row, side).wait_send()

    below(left, 0)
    for i in range(2):
        part_copy(i).wait_send()

    @pl.when(early)
    def _():
        for target in range(ne):
            @pl.when(target != z)
            def _():
                z_copy(target).wait_send()
        for target in edges[1]:
            z_copy(target).wait_send()

    @pl.when(jnp.logical_not(early))
    def _():
        z_copy(len(edges[0]) - 1).wait_send()
        for target in range(ne, nz):
            @pl.when(target != z)
            def _():
                z_copy(target).wait_send()
    for by, of, target, lane in routes:
        @pl.when(z == by)
        def _():
            pass_copy(of, target, lane).wait_send()
    rest_copy.wait()


def per_device(nx, queries, keys, values, vertical, slash, plan):
    nz = lax.axis_size("head") // 2
    ny = lax.axis_size("seq") // nx
    nb = ny * nx
    rows = GROUP * BLK
    mine = OWN * BLK
    bf, f32 = jnp.bfloat16, jnp.float32
    hbm = pl.BlockSpec(memory_space=pltpu.HBM)
    dma = pltpu.SemaphoreType.DMA
    tables = (vertical.shape[1], vertical.shape[0])
    out, rest = pl.pallas_call(
        functools.partial(kernel, ny, nx, nz),
        out_shape=[pltpu.VMEM((BLK, OWN * HD), bf)] * 2,
        in_specs=[hbm] * 6,
        out_specs=[pl.BlockSpec(memory_space=pltpu.VMEM)] * 2,
        scratch_shapes=[
            pltpu.SMEM(plan.shape, jnp.int32),
            pltpu.VMEM(tables, jnp.int32),
            pltpu.VMEM(tables, jnp.int32),
            pltpu.VMEM((nb, 2, HALF, HD), bf),
            pltpu.VMEM((2, BLK, OWN * HD), bf),
            pltpu.VMEM((rows, HD), bf),
            pltpu.VMEM((ny, nx, 1, rows), f32),
            pltpu.VMEM((1, rows), f32),
            pltpu.VMEM((1, rows), f32),
            pltpu.VMEM((2, HD + 16, mine), f32),
            pltpu.VMEM((HD + 16, mine), f32),
            pltpu.VMEM((nz, OWN, BLK, HD), bf),
            pltpu.VMEM((BLK, OWN * HD), bf),
            dma((6,)),
            dma((ny,)),
            dma((ny,)),
            dma((1,)),
            dma((ny, 2)),
            dma((nb,)),
            dma((2,)),
            dma((2, 2)),
            dma((nz,)),
            dma((2, nz)),
            dma((nz,)),
            dma((2,)),
            pltpu.SemaphoreType.REGULAR((nz,)),
        ],
        compiler_params=pltpu.CompilerParams(
            collective_id=0, has_side_effects=True, vmem_limit_bytes=60 * 2**20),
    )(plan, vertical.T, slash.T, queries, keys, values)
    return out + rest


def solution(mesh, nx=NX):
    in_specs = (P("seq", "head"), P("seq", None), P("seq", None), P(), P(), P())
    return jax.shard_map(
        functools.partial(per_device, nx), mesh=mesh, in_specs=in_specs,
        out_specs=P("seq", "head"), check_vma=False)
```

```python
import functools

import jax
import jax.numpy as jnp
from jax import lax
from jax.experimental import pallas as pl
from jax.experimental.pallas import tpu as pltpu
from jax.sharding import PartitionSpec as P

HD = 128
BLK = 64
HALF = BLK // 2
NX = 4
GROUP = 8
OWN = 4
PIECES = 2
LOW = -1e30
SCALE2 = (HD**-0.5) * 1.4426950408889634
MESH = pl.DeviceIdType.MESH


def kernel(
    ny, nx, nz,
    plan_hbm, vertical_hbm, slash_hbm, queries, keys, values, out, rest,
    plan, vertical, slash, kvb, qb, qs, bias, top, total, part, got, gath, pick,
    in_sem, y_send, far_send, across_send, x_send, kv_recv, q_sem, part_sem, z_send, pass_send, z_recv, rest_sem, late,
):
    s = lax.axis_index("seq")
    h = lax.axis_index("head")
    y, x = s // nx, s % nx
    z, core = h // 2, h % 2
    sib = z * 2 + (1 - core)
    ne = nz // 2
    early = z < ne
    rows = GROUP * BLK
    mine = OWN * BLK
    chunk = nx * HALF
    sides = [t for t in sorted({1, nx - 1}) if t % nx]
    across = nx // 2 if nx > 2 else 0

    def signal(where, device):
        pl.semaphore_signal(where, inc=1, device_id=device, device_id_type=MESH)

    def remote(src, dst, send, recv, device):
        return pltpu.make_async_remote_copy(
            src_ref=src, dst_ref=dst, send_sem=send, recv_sem=recv, device_id=device, device_id_type=MESH)

    column = pl.ds(pl.multiple_of(z * HD, HD), HD)
    half = pl.ds(pl.multiple_of(core * HALF, HALF), HALF)
    k_load = pltpu.make_async_copy(keys.at[half, column], kvb.at[s, 0], in_sem.at[0])
    v_load = pltpu.make_async_copy(values.at[half, column], kvb.at[s, 1], in_sem.at[1])
    q_load = pltpu.make_async_copy(queries, qb.at[core], in_sem.at[2])
    plan_load = pltpu.make_async_copy(plan_hbm, plan, in_sem.at[3])
    vert_load = pltpu.make_async_copy(vertical_hbm, vertical, in_sem.at[4])
    slash_load = pltpu.make_async_copy(slash_hbm, slash, in_sem.at[5])
    loads = [k_load, v_load, q_load, vert_load, slash_load, plan_load]
    barrier = pltpu.get_barrier_semaphore()
    def greet(row, carry):
        signal(barrier, (row * nx + x, h))
        return carry

    lax.fori_loop(0, y, greet, 0)
    partners = [(y * nx + (x + t) % nx, h) for t in range(1, nx)]
    partners += [(s, sib)]
    for partner in partners:
        signal(barrier, partner)
    for other in range(1, nz):
        @pl.when(other > z)
        def _():
            signal(barrier, (s, other * 2 + core))
    for load in loads:
        load.start()
    pl.semaphore_wait(barrier, len(partners) + ny - 1 - y + z)

    def y_copy(t):
        return remote(kvb.at[s], kvb.at[s], y_send.at[t - 1], kv_recv.at[s], ((y + t) * nx + x, h))

    over = y * nx + (x + across) % nx

    def far_copy(t):
        return remote(kvb.at[over], kvb.at[over], far_send.at[t - 1], kv_recv.at[over], ((y + t) * nx + x, h))

    across_copy = remote(kvb.at[s], kvb.at[s], across_send.at[0], kv_recv.at[s], (over, h))

    def x_copy(row, side):
        b = row * nx + x
        to = (x + sides[side]) % nx
        return remote(kvb.at[b], kvb.at[b], x_send.at[row, side], kv_recv.at[b], (y * nx + to, h))

    def block_wait(b):
        remote(kvb.at[b], kvb.at[b], y_send.at[0], kv_recv.at[b], (s, sib)).wait_recv()

    def above(action):
        def step(i, carry):
            action(ny - 1 - y - i)
            return carry

        lax.fori_loop(0, ny - 1 - y, step, 0)

    def below(action, first):
        def step(i, carry):
            t = jnp.where(i % 2 == 1, (i + 1) // 2, ny - i // 2) % ny

            @pl.when(t <= y)
            def _():
                action(y - t)

            return carry

        lax.fori_loop(first, ny, step, 0)

    k_load.wait()
    v_load.wait()
    if across:
        across_copy.start()
    above(lambda t: y_copy(t).start())
    for side in range(len(sides)):
        x_copy(y, side).start()
    q_load.wait()
    q_copy = remote(qb.at[core], qb.at[core], q_sem.at[0], q_sem.at[1], (s, sib))
    q_copy.start()
    for other in range(nz - 1):
        @pl.when(other < z)
        def _():
            signal(late.at[z], (s, other * 2 + core))

    vert_load.wait()
    slash_load.wait()
    heads = vertical.shape[1]
    spread = (
        lax.broadcasted_iota(jnp.int32, (heads, rows), 0)
        == z * GROUP + lax.broadcasted_iota(jnp.int32, (heads, rows), 1) // BLK
    ).astype(jnp.float32)
    blocks = lax.broadcasted_iota(jnp.int32, (ny * nx, heads), 0)
    hit = blocks < 0
    for n in range(vertical.shape[0]):
        hit = hit | (blocks == vertical[n : n + 1, :])
    for n in range(slash.shape[0]):
        hit = hit | (s - blocks == slash[n : n + 1, :])
    open_ = jnp.where(hit & (blocks <= s), 1.0, 0.0)
    open_rows = jnp.dot(open_, spread, preferred_element_type=jnp.float32)
    bias[...] = jnp.where(open_rows > 0.5, 0.0, LOW).reshape(ny, nx, 1, rows)
    top[...] = jnp.full_like(top, LOW)
    total[...] = jnp.zeros_like(total)
    part[...] = jnp.zeros_like(part)

    if across:
        @pl.when(core == 0)
        def _():
            block_wait(over)
            above(lambda t: far_copy(t).start())

    def wide_copy(row):
        b = row * nx + x
        return remote(kvb.at[b], kvb.at[b], far_send.at[row], kv_recv.at[b], (over, h))

    def forward(row):
        block_wait(row * nx + x)
        if across:
            @pl.when(core == 1)
            def _():
                wide_copy(row).start()
        for side in range(len(sides)):
            x_copy(row, side).start()

    below(forward, 1)

    q_copy.wait()
    for i in range(GROUP):
        qs[i * BLK : (i + 1) * BLK, :] = qb[i // OWN, :, (i % OWN) * HD : (i % OWN + 1) * HD]

    def attend(row, diagonal):
        these = pl.ds(row * nx, nx)
        k_rows = kvb[these, 0].reshape(chunk, HD)
        v_rows = kvb[these, 1].reshape(chunk, HD)
        v_turned = v_rows.astype(jnp.float32).T.astype(jnp.bfloat16)
        raw = lax.dot_general(
            k_rows, qs[...], (((1,), (1,)), ((), ())), preferred_element_type=jnp.float32)
        shape = (nx, HALF, rows)
        raw = raw.reshape(shape) + bias[row]
        if diagonal:
            key_at = (
                (row * nx + lax.broadcasted_iota(jnp.int32, shape, 0)) * BLK
                + core * HALF + lax.broadcasted_iota(jnp.int32, shape, 1))
            query_at = s * BLK + lax.broadcasted_iota(jnp.int32, shape, 2) % BLK
            raw = jnp.where(key_at <= query_at, raw, LOW)
        raw = raw.reshape(chunk, rows)
        old = top[...]
        new = jnp.maximum(old, jnp.max(raw, axis=0, keepdims=True))
        w = jnp.exp2((raw - new) * SCALE2)
        keep = jnp.exp2((old - new) * SCALE2)
        top[...] = new
        total[...] = total[...] * keep + jnp.sum(w, axis=0, keepdims=True)
        more = jnp.dot(v_turned, w.astype(jnp.bfloat16), preferred_element_type=jnp.float32)
        for c in range(2):
            lanes = slice(c * mine, (c + 1) * mine)
            part[c, :HD, :] = part[c, :HD, :] * keep[:, lanes] + more[:, lanes]

    def one_row(row, diagonal=False):
        for u in sides:
            block_wait(row * nx + (x + u) % nx)
        if across:
            @pl.when((row < y) | (core == 1))
            def _():
                block_wait(row * nx + (x + across) % nx)
        attend(row, diagonal)

    one_row(y, True)
    below(one_row, 1)

    for c in range(2):
        lanes = slice(c * mine, (c + 1) * mine)
        part[c, HD : HD + 8, :] = jnp.broadcast_to(top[:, lanes], (8, mine))
        part[c, HD + 8 :, :] = jnp.broadcast_to(total[:, lanes], (8, mine))
    def part_copy(i):
        lanes = pl.ds(i * (mine // 2), mine // 2)
        return remote(part.at[1 - core, :, lanes], got.at[:, lanes], part_sem.at[0, i], part_sem.at[1, i], (s, sib))

    width = OWN // PIECES

    def send(source, target, sem, piece):
        block = gath.at[source, pl.ds(piece * width, width)]
        return remote(block, block, sem, z_recv.at[source, piece], (s, target * 2 + core))

    high = z >= nz - ne // 2
    nearer = jnp.where(high, 0, ne - 1)

    for i in range(2):
        part_copy(i).start()
    for i in range(2):
        lanes = slice(i * (mine // 2), (i + 1) * (mine // 2))
        part_copy(i).wait_recv()
        top_a, top_b = part[core, HD : HD + 1, lanes], got[HD : HD + 1, lanes]
        both = jnp.maximum(top_a, top_b)
        scale_a = jnp.exp2((top_a - both) * SCALE2)
        scale_b = jnp.exp2((top_b - both) * SCALE2)
        under = part[core, HD + 8 : HD + 9, lanes] * scale_a + got[HD + 8 : HD + 9, lanes] * scale_b
        mixed = part[core, :HD, lanes] * (scale_a / under) + got[:HD, lanes] * (scale_b / under)
        gath[z, i * 2 : i * 2 + 2] = mixed.T.astype(jnp.bfloat16).reshape(2, BLK, HD)

        @pl.when(jnp.logical_not(early))
        def _():
            send(z, nearer, z_send.at[0, i], i).start()

    top_edge, low_edge = nz - 1, ne
    edges = [sorted({0, ne - 1}), sorted({low_edge, top_edge})]
    passes = ne >= 4
    upper = range(nz - ne // 2, nz) if passes else []
    lower = [source for source in range(ne, nz) if source not in upper]

    def z_start(target, slot):
        for piece in range(PIECES):
            send(z, target, z_send.at[slot, piece], piece).start()

    def z_left(slot):
        for piece in range(PIECES):
            send(z, 0, z_send.at[slot, piece], piece).wait_send()

    def pass_copy(source, target, lane, piece):
        return send(source, target, pass_send.at[lane, source, piece], piece)

    def late_wait(target):
        @pl.when(target > z)
        def _():
            pl.semaphore_wait(late.at[target], 1)

    def arrive(source, piece):
        @pl.when(source != z)
        def _():
            pass_copy(source, 0, 0, piece).wait_recv()

    routes = []
    if passes:
        for source in upper:
            routes += [(0, source, 1, 0), (0, source, ne - 2, 1)]
        for source in lower:
            routes += [(ne - 1, source, ne - 2, 0), (ne - 1, source, 1, 1)]
        routes += [(top_edge, source, top_edge - 1, 0) for source in range(ne)]
        routes += [(low_edge, source, low_edge + 1, 0) for source in range(ne)]

    def relay(plane, order):
        pairs = [order[i : i + 2] for i in range(0, len(order), 2)]

        @pl.when(z == plane)
        def _():
            for pair in pairs:
                for piece in range(PIECES):
                    for source in pair:
                        arrive(source, piece)
                        for by, of, target, lane in routes:
                            if by == plane and of == source:
                                pass_copy(source, target, lane, piece).start()

    @pl.when(early)
    def _():
        for target in range(ne):
            late_wait(target)

            @pl.when(target != z)
            def _():
                z_start(target, target)
        for target in reversed(range(ne, nz)):
            late_wait(target)
            if target in edges[1]:
                z_start(target, target)
        for source in range(ne):
            for piece in range(PIECES):
                arrive(source, piece)
        relay(0, list(reversed(range(ne, nz))))
        for plane in range(1, ne):
            relay(plane, list(range(ne, nz)))

    @pl.when(jnp.logical_not(early))
    def _():
        if len(edges[0]) == 2:
            second = ne - 1 - nearer
            for target in range(ne, nz):
                late_wait(target)

                @pl.when(target != z)
                def _():
                    z_start(target, target)
            z_left(0)
            z_start(second, 1)
        for plane in range(ne, nz):
            relay(plane, list(range(ne)))
        for source in range(ne, nz):
            for piece in range(PIECES):
                arrive(source, piece)

    plan_load.wait()

    def collect(into, device):
        for t in range(OWN):
            head = plan[device * OWN + t]
            item = gath[head // GROUP, head % OWN]
            into[:, t * HD : (t + 1) * HD] = jnp.where((head // OWN) % 2 == core, item, jnp.zeros_like(item))

    collect(pick, sib)
    rest_copy = remote(pick, rest, rest_sem.at[0], rest_sem.at[1], (s, sib))
    rest_copy.start()
    collect(out, h)

    if across:
        across_copy.wait_send()
    above(lambda t: y_copy(t).wait_send())
    if across:
        @pl.when(core == 0)
        def _():
            above(lambda t: far_copy(t).wait_send())

        @pl.when(core == 1)
        def _():
            below(lambda row: wide_copy(row).wait_send(), 1)

    def left(row):
        for side in range(len(sides)):
            x_copy(row, side).wait_send()

    below(left, 0)
    for i in range(2):
        part_copy(i).wait_send()

    @pl.when(early)
    def _():
        for target in range(ne):
            @pl.when(target != z)
            def _():
                z_left(target)
        for target in edges[1]:
            z_left(target)

    @pl.when(jnp.logical_not(early))
    def _():
        z_left(len(edges[0]) - 1)
        for target in range(ne, nz):
            @pl.when(target != z)
            def _():
                z_left(target)
    for by, of, target, lane in routes:
        @pl.when(z == by)
        def _():
            for piece in range(PIECES):
                pass_copy(of, target, lane, piece).wait_send()
    rest_copy.wait()


def per_device(nx, queries, keys, values, vertical, slash, plan):
    nz = lax.axis_size("head") // 2
    ny = lax.axis_size("seq") // nx
    nb = ny * nx
    rows = GROUP * BLK
    mine = OWN * BLK
    bf, f32 = jnp.bfloat16, jnp.float32
    hbm = pl.BlockSpec(memory_space=pltpu.HBM)
    dma = pltpu.SemaphoreType.DMA
    tables = (vertical.shape[1], vertical.shape[0])
    out, rest = pl.pallas_call(
        functools.partial(kernel, ny, nx, nz),
        out_shape=[pltpu.VMEM((BLK, OWN * HD), bf)] * 2,
        in_specs=[hbm] * 6,
        out_specs=[pl.BlockSpec(memory_space=pltpu.VMEM)] * 2,
        scratch_shapes=[
            pltpu.SMEM(plan.shape, jnp.int32),
            pltpu.VMEM(tables, jnp.int32),
            pltpu.VMEM(tables, jnp.int32),
            pltpu.VMEM((nb, 2, HALF, HD), bf),
            pltpu.VMEM((2, BLK, OWN * HD), bf),
            pltpu.VMEM((rows, HD), bf),
            pltpu.VMEM((ny, nx, 1, rows), f32),
            pltpu.VMEM((1, rows), f32),
            pltpu.VMEM((1, rows), f32),
            pltpu.VMEM((2, HD + 16, mine), f32),
            pltpu.VMEM((HD + 16, mine), f32),
            pltpu.VMEM((nz, OWN, BLK, HD), bf),
            pltpu.VMEM((BLK, OWN * HD), bf),
            dma((6,)),
            dma((ny,)),
            dma((ny,)),
            dma((1,)),
            dma((ny, 2)),
            dma((nb,)),
            dma((2,)),
            dma((2, 2)),
            dma((nz, PIECES)),
            dma((2, nz, PIECES)),
            dma((nz, PIECES)),
            dma((2,)),
            pltpu.SemaphoreType.REGULAR((nz,)),
        ],
        compiler_params=pltpu.CompilerParams(
            collective_id=0, has_side_effects=True, vmem_limit_bytes=60 * 2**20),
    )(plan, vertical.T, slash.T, queries, keys, values)
    return out + rest


def solution(mesh, nx=NX):
    in_specs = (P("seq", "head"), P("seq", None), P("seq", None), P(), P(), P())
    return jax.shard_map(
        functools.partial(per_device, nx), mesh=mesh, in_specs=in_specs,
        out_specs=P("seq", "head"), check_vma=False)
```

```python
import functools

import jax
import jax.numpy as jnp
from jax import lax
from jax.experimental import pallas as pl
from jax.experimental.pallas import tpu as pltpu
from jax.sharding import PartitionSpec as P

HD = 128
BLK = 64
HALF = BLK // 2
NX = 4
GROUP = 8
OWN = 4
LOW = -1e30
SCALE2 = (HD**-0.5) * 1.4426950408889634
MESH = pl.DeviceIdType.MESH


def kernel(
    ny, nx, nz,
    plan_hbm, vertical_hbm, slash_hbm, queries, keys, values, out, rest,
    plan, vertical, slash, kvb, qb, qs, bias, top, total, part, got, gath, pick,
    in_sem, y_send, far_send, across_send, x_send, kv_recv, q_sem, part_sem, z_send, pass_send, z_recv, rest_sem, late,
):
    s = lax.axis_index("seq")
    h = lax.axis_index("head")
    y, x = s // nx, s % nx
    z, core = h // 2, h % 2
    sib = z * 2 + (1 - core)
    ne = nz // 2
    early = z < ne
    rows = GROUP * BLK
    mine = OWN * BLK
    chunk = nx * HALF
    sides = [t for t in sorted({1, nx - 1}) if t % nx]
    across = nx // 2 if nx > 2 else 0

    def signal(where, device):
        pl.semaphore_signal(where, inc=1, device_id=device, device_id_type=MESH)

    def remote(src, dst, send, recv, device):
        return pltpu.make_async_remote_copy(
            src_ref=src, dst_ref=dst, send_sem=send, recv_sem=recv, device_id=device, device_id_type=MESH)

    column = pl.ds(pl.multiple_of(z * HD, HD), HD)
    half = pl.ds(pl.multiple_of(core * HALF, HALF), HALF)
    k_load = pltpu.make_async_copy(keys.at[half, column], kvb.at[s, 0], in_sem.at[0])
    v_load = pltpu.make_async_copy(values.at[half, column], kvb.at[s, 1], in_sem.at[1])
    q_load = pltpu.make_async_copy(queries, qb.at[core], in_sem.at[2])
    plan_load = pltpu.make_async_copy(plan_hbm, plan, in_sem.at[3])
    vert_load = pltpu.make_async_copy(vertical_hbm, vertical, in_sem.at[4])
    slash_load = pltpu.make_async_copy(slash_hbm, slash, in_sem.at[5])
    loads = [k_load, v_load, q_load, vert_load, slash_load, plan_load]
    barrier = pltpu.get_barrier_semaphore()
    def greet(row, carry):
        signal(barrier, (row * nx + x, h))
        return carry

    lax.fori_loop(0, y, greet, 0)
    partners = [(y * nx + (x + t) % nx, h) for t in range(1, nx)]
    partners += [(s, sib)]
    for partner in partners:
        signal(barrier, partner)
    for other in range(1, nz):
        @pl.when(other > z)
        def _():
            signal(barrier, (s, other * 2 + core))
    for load in loads:
        load.start()
    pl.semaphore_wait(barrier, len(partners) + ny - 1 - y + z)

    def y_copy(t):
        return remote(kvb.at[s], kvb.at[s], y_send.at[t - 1], kv_recv.at[s], ((y + t) * nx + x, h))

    over = y * nx + (x + across) % nx

    def far_copy(t):
        return remote(kvb.at[over], kvb.at[over], far_send.at[t - 1], kv_recv.at[over], ((y + t) * nx + x, h))

    across_copy = remote(kvb.at[s], kvb.at[s], across_send.at[0], kv_recv.at[s], (over, h))

    def x_copy(row, side):
        b = row * nx + x
        to = (x + sides[side]) % nx
        return remote(kvb.at[b], kvb.at[b], x_send.at[row, side], kv_recv.at[b], (y * nx + to, h))

    def block_wait(b):
        remote(kvb.at[b], kvb.at[b], y_send.at[0], kv_recv.at[b], (s, sib)).wait_recv()

    def above(action):
        def step(i, carry):
            action(ny - 1 - y - i)
            return carry

        lax.fori_loop(0, ny - 1 - y, step, 0)

    def below(action, first):
        def step(i, carry):
            t = jnp.where(i % 2 == 1, (i + 1) // 2, ny - i // 2) % ny

            @pl.when(t <= y)
            def _():
                action(y - t)

            return carry

        lax.fori_loop(first, ny, step, 0)

    k_load.wait()
    v_load.wait()
    if across:
        across_copy.start()
    above(lambda t: y_copy(t).start())
    for side in range(len(sides)):
        x_copy(y, side).start()
    q_load.wait()
    q_copy = remote(qb.at[core], qb.at[core], q_sem.at[0], q_sem.at[1], (s, sib))
    q_copy.start()
    for other in range(nz - 1):
        @pl.when(other < z)
        def _():
            signal(late.at[z], (s, other * 2 + core))

    vert_load.wait()
    slash_load.wait()
    heads = vertical.shape[1]
    spread = (
        lax.broadcasted_iota(jnp.int32, (heads, rows), 0)
        == z * GROUP + lax.broadcasted_iota(jnp.int32, (heads, rows), 1) // BLK
    ).astype(jnp.float32)
    blocks = lax.broadcasted_iota(jnp.int32, (ny * nx, heads), 0)
    hit = blocks < 0
    for n in range(vertical.shape[0]):
        hit = hit | (blocks == vertical[n : n + 1, :])
    for n in range(slash.shape[0]):
        hit = hit | (s - blocks == slash[n : n + 1, :])
    open_ = jnp.where(hit & (blocks <= s), 1.0, 0.0)
    open_rows = jnp.dot(open_, spread, preferred_element_type=jnp.float32)
    bias[...] = jnp.where(open_rows > 0.5, 0.0, LOW).reshape(ny, nx, 1, rows)
    top[...] = jnp.full_like(top, LOW)
    total[...] = jnp.zeros_like(total)
    part[...] = jnp.zeros_like(part)

    if across:
        @pl.when(core == 0)
        def _():
            block_wait(over)
            above(lambda t: far_copy(t).start())

    def wide_copy(row):
        b = row * nx + x
        return remote(kvb.at[b], kvb.at[b], far_send.at[row], kv_recv.at[b], (over, h))

    def forward(row):
        block_wait(row * nx + x)
        if across:
            @pl.when(core == 1)
            def _():
                wide_copy(row).start()
        for side in range(len(sides)):
            x_copy(row, side).start()

    below(forward, 1)

    q_copy.wait()
    for i in range(GROUP):
        qs[i * BLK : (i + 1) * BLK, :] = qb[i // OWN, :, (i % OWN) * HD : (i % OWN + 1) * HD]

    def attend(row, diagonal):
        these = pl.ds(row * nx, nx)
        k_rows = kvb[these, 0].reshape(chunk, HD)
        v_rows = kvb[these, 1].reshape(chunk, HD)
        v_turned = v_rows.astype(jnp.float32).T.astype(jnp.bfloat16)
        raw = lax.dot_general(
            k_rows, qs[...], (((1,), (1,)), ((), ())), preferred_element_type=jnp.float32)
        shape = (nx, HALF, rows)
        raw = raw.reshape(shape) + bias[row]
        if diagonal:
            key_at = (
                (row * nx + lax.broadcasted_iota(jnp.int32, shape, 0)) * BLK
                + core * HALF + lax.broadcasted_iota(jnp.int32, shape, 1))
            query_at = s * BLK + lax.broadcasted_iota(jnp.int32, shape, 2) % BLK
            raw = jnp.where(key_at <= query_at, raw, LOW)
        raw = raw.reshape(chunk, rows)
        old = top[...]
        new = jnp.maximum(old, jnp.max(raw, axis=0, keepdims=True))
        w = jnp.exp2((raw - new) * SCALE2)
        keep = jnp.exp2((old - new) * SCALE2)
        top[...] = new
        total[...] = total[...] * keep + jnp.sum(w, axis=0, keepdims=True)
        more = jnp.dot(v_turned, w.astype(jnp.bfloat16), preferred_element_type=jnp.float32)
        for c in range(2):
            lanes = slice(c * mine, (c + 1) * mine)
            part[c, :HD, :] = part[c, :HD, :] * keep[:, lanes] + more[:, lanes]

    def one_row(row, diagonal=False):
        for u in sides:
            block_wait(row * nx + (x + u) % nx)
        if across:
            @pl.when((row < y) | (core == 1))
            def _():
                block_wait(row * nx + (x + across) % nx)
        attend(row, diagonal)

    one_row(y, True)
    below(one_row, 1)

    for c in range(2):
        lanes = slice(c * mine, (c + 1) * mine)
        part[c, HD : HD + 8, :] = jnp.broadcast_to(top[:, lanes], (8, mine))
        part[c, HD + 8 :, :] = jnp.broadcast_to(total[:, lanes], (8, mine))
    def part_copy(i):
        lanes = pl.ds(i * (mine // 2), mine // 2)
        return remote(part.at[1 - core, :, lanes], got.at[:, lanes], part_sem.at[0, i], part_sem.at[1, i], (s, sib))

    for i in range(2):
        part_copy(i).start()
    for i in range(2):
        lanes = slice(i * (mine // 2), (i + 1) * (mine // 2))
        part_copy(i).wait_recv()
        top_a, top_b = part[core, HD : HD + 1, lanes], got[HD : HD + 1, lanes]
        both = jnp.maximum(top_a, top_b)
        scale_a = jnp.exp2((top_a - both) * SCALE2)
        scale_b = jnp.exp2((top_b - both) * SCALE2)
        under = part[core, HD + 8 : HD + 9, lanes] * scale_a + got[HD + 8 : HD + 9, lanes] * scale_b
        mixed = part[core, :HD, lanes] * (scale_a / under) + got[:HD, lanes] * (scale_b / under)
        gath[z, i * 2 : i * 2 + 2] = mixed.T.astype(jnp.bfloat16).reshape(2, BLK, HD)

    top_edge, low_edge = nz - 1, ne
    edges = [sorted({0, ne - 1}), sorted({low_edge, top_edge})]
    passes = ne >= 4
    upper = range(nz - ne // 2, nz) if passes else []
    lower = [source for source in range(ne, nz) if source not in upper]

    def send(source, target, sem):
        return remote(gath.at[source], gath.at[source], sem, z_recv.at[source], (s, target * 2 + core))

    def z_copy(target):
        return send(z, target, z_send.at[target])

    def pass_copy(source, target, lane=0):
        return send(source, target, pass_send.at[lane, source])

    def late_wait(target):
        @pl.when(target > z)
        def _():
            pl.semaphore_wait(late.at[target], 1)

    def arrive(source):
        @pl.when(source != z)
        def _():
            pass_copy(source, 0).wait_recv()

    routes = []
    if passes:
        for source in upper:
            routes += [(0, source, 1, 0), (0, source, ne - 2, 1)]
        for source in lower:
            routes += [(ne - 1, source, 1, 1), (ne - 1, source, ne - 2, 0)]
        routes += [(top_edge, source, top_edge - 1, 0) for source in range(ne)]
        routes += [(low_edge, source, low_edge + 1, 0) for source in range(ne)]

    def relay(plane, order):
        @pl.when(z == plane)
        def _():
            for source in order:
                arrive(source)
                for by, of, target, lane in routes:
                    if by == plane and of == source:
                        pass_copy(source, target, lane).start()

    @pl.when(early)
    def _():
        for target in range(ne):
            late_wait(target)

            @pl.when(target != z)
            def _():
                z_copy(target).start()
        for target in reversed(range(ne, nz)):
            late_wait(target)
            if target in edges[1]:
                z_copy(target).start()
        for source in range(ne):
            arrive(source)
        relay(0, list(reversed(range(ne, nz))))
        for plane in range(1, ne):
            relay(plane, list(range(ne, nz)))

    @pl.when(jnp.logical_not(early))
    def _():
        high = z >= nz - ne // 2
        if len(edges[0]) == 2:
            first = jnp.where(high, 0, ne - 1)
            second = ne - 1 - first
            send(z, first, z_send.at[0]).start()
            for target in range(ne, nz):
                late_wait(target)

                @pl.when(target != z)
                def _():
                    z_copy(target).start()
            z_copy(0).wait_send()
            send(z, second, z_send.at[1]).start()
        else:
            send(z, 0, z_send.at[0]).start()
        for plane in range(ne, nz):
            relay(plane, list(range(ne)))
        for source in range(ne, nz):
            arrive(source)

    plan_load.wait()

    def collect(into, device):
        for t in range(OWN):
            head = plan[device * OWN + t]
            item = gath[head // GROUP, head % OWN]
            into[:, t * HD : (t + 1) * HD] = jnp.where((head // OWN) % 2 == core, item, jnp.zeros_like(item))

    collect(pick, sib)
    rest_copy = remote(pick, rest, rest_sem.at[0], rest_sem.at[1], (s, sib))
    rest_copy.start()
    collect(out, h)

    if across:
        across_copy.wait_send()
    above(lambda t: y_copy(t).wait_send())
    if across:
        @pl.when(core == 0)
        def _():
            above(lambda t: far_copy(t).wait_send())

        @pl.when(core == 1)
        def _():
            below(lambda row: wide_copy(row).wait_send(), 1)

    def left(row):
        for side in range(len(sides)):
            x_copy(row, side).wait_send()

    below(left, 0)
    for i in range(2):
        part_copy(i).wait_send()

    @pl.when(early)
    def _():
        for target in range(ne):
            @pl.when(target != z)
            def _():
                z_copy(target).wait_send()
        for target in edges[1]:
            z_copy(target).wait_send()

    @pl.when(jnp.logical_not(early))
    def _():
        z_copy(len(edges[0]) - 1).wait_send()
        for target in range(ne, nz):
            @pl.when(target != z)
            def _():
                z_copy(target).wait_send()
    for by, of, target, lane in routes:
        @pl.when(z == by)
        def _():
            pass_copy(of, target, lane).wait_send()
    rest_copy.wait()


def per_device(nx, queries, keys, values, vertical, slash, plan):
    nz = lax.axis_size("head") // 2
    ny = lax.axis_size("seq") // nx
    nb = ny * nx
    rows = GROUP * BLK
    mine = OWN * BLK
    bf, f32 = jnp.bfloat16, jnp.float32
    hbm = pl.BlockSpec(memory_space=pltpu.HBM)
    dma = pltpu.SemaphoreType.DMA
    tables = (vertical.shape[1], vertical.shape[0])
    out, rest = pl.pallas_call(
        functools.partial(kernel, ny, nx, nz),
        out_shape=[pltpu.VMEM((BLK, OWN * HD), bf)] * 2,
        in_specs=[hbm] * 6,
        out_specs=[pl.BlockSpec(memory_space=pltpu.VMEM)] * 2,
        scratch_shapes=[
            pltpu.SMEM(plan.shape, jnp.int32),
            pltpu.VMEM(tables, jnp.int32),
            pltpu.VMEM(tables, jnp.int32),
            pltpu.VMEM((nb, 2, HALF, HD), bf),
            pltpu.VMEM((2, BLK, OWN * HD), bf),
            pltpu.VMEM((rows, HD), bf),
            pltpu.VMEM((ny, nx, 1, rows), f32),
            pltpu.VMEM((1, rows), f32),
            pltpu.VMEM((1, rows), f32),
            pltpu.VMEM((2, HD + 16, mine), f32),
            pltpu.VMEM((HD + 16, mine), f32),
            pltpu.VMEM((nz, OWN, BLK, HD), bf),
            pltpu.VMEM((BLK, OWN * HD), bf),
            dma((6,)),
            dma((ny,)),
            dma((ny,)),
            dma((1,)),
            dma((ny, 2)),
            dma((nb,)),
            dma((2,)),
            dma((2, 2)),
            dma((nz,)),
            dma((2, nz)),
            dma((nz,)),
            dma((2,)),
            pltpu.SemaphoreType.REGULAR((nz,)),
        ],
        compiler_params=pltpu.CompilerParams(
            collective_id=0, has_side_effects=True, vmem_limit_bytes=60 * 2**20),
    )(plan, vertical.T, slash.T, queries, keys, values)
    return out + rest


def solution(mesh, nx=NX):
    in_specs = (P("seq", "head"), P("seq", None), P("seq", None), P(), P(), P())
    return jax.shard_map(
        functools.partial(per_device, nx), mesh=mesh, in_specs=in_specs,
        out_specs=P("seq", "head"), check_vma=False)
```
